256 devices in a mesh: grp: 4 (over x_hi, core), ctx: 64 (over x_lo, z, y).
Axes of the slice: x: 4 (x_hi: 2, x_lo: 2; x = x_hi * 2 + x_lo), y: 4, z: 8, core: 2. Of those that a mesh axis runs over, the one named last changes fastest.
Arguments:
- queries: bfloat16 [65536, 28, 128], P(('grp', 'ctx')), may hold values from -12 to 12
- key_rows: bfloat16 [65536, 4, 128], P(('grp', 'ctx')), may hold values from -6 to 6
- value_rows: bfloat16 [65536, 4, 128], P(('grp', 'ctx')), may hold values from -6 to 6
- out_grad: bfloat16 [65536, 28, 128], P(('grp', 'ctx')), may hold values from -6 to 6
- doc_ids: int32 [65536], P(('grp', 'ctx')), may hold values from 0 to 127, never falling along the last dimension, each value on 1 to 768 neighbouring positions
Outputs:
- query_grad: bfloat16 [65536, 28, 128], P(('grp', 'ctx'))
- key_grad: bfloat16 [65536, 4, 128], P(('grp', 'ctx'))
- value_grad: bfloat16 [65536, 4, 128], P(('grp', 'ctx'))
The draws below stay inside these ranges and needn't reach their ends.
Inputs may be any that keep to these rules, and one draw needn't show every extreme that they name: `doc_ids`: document numbers never fall along the tokens; every document has 1 to 768 tokens, and one has exactly 768.
All inputs are finite; a program needn't handle non-finite values.
Results may differ from the reference program's by a relative error of at most 0.0074.
Values may be sent and summed in bfloat16 or wider, within the bound.
A program may use at most 192 MiB of HBM per device.

```python
import math
import jax
import jax.numpy as jnp
import numpy as np
from jax import lax

QH = 28
KVH = 4
HD = 128
TOK_DEV = 256
REACH = 3
TOKENS = 65536
MOST = 768
DOCS = 128


def draw_queries(key, part):
    key = jax.random.fold_in(key, 1)
    drawn = jnp.clip(jax.random.normal(key, (TOKENS, QH, HD), jnp.float32), -6.0, 6.0)
    return drawn.astype(jnp.bfloat16)


def draw_key_rows(key, part):
    key = jax.random.fold_in(key, 2)
    drawn = jnp.clip(jax.random.normal(key, (TOKENS, KVH, HD), jnp.float32), -6.0, 6.0)
    return drawn.astype(jnp.bfloat16)


def block_levels(rng, extent, split, least, largest):
    level = 1.0
    for axis_at, shards_of in split:
        draws = jax.random.uniform(jax.random.fold_in(jax.random.fold_in(rng, 6), axis_at), (shards_of,), jnp.float32, least / len(split), largest / len(split))
        level = level * jnp.repeat(jnp.exp(draws), extent[axis_at] // shards_of).reshape((-1,) + (1,) * (len(extent) - 1 - axis_at))
    return level


def length_profile(count, total, bound, skew):
    loads = [(1 << 20) // math.isqrt(grade ** skew) + 1 for grade in range(2, count + 1)]
    surplus, given = total - bound - (count - 1), [1] * (count - 1)
    while surplus > 0:
        movable = [i for i in range(count - 1) if given[i] < bound]
        mass, budget = sum([loads[i] for i in movable]), surplus
        for i in movable:
            more = min(bound - given[i], max(1, budget * loads[i] // mass), surplus)
            given[i] = given[i] + more
            surplus = surplus - more
    return np.array([bound] + given)


def ragged_sizes(own_key, amount, total, most, slope):
    if amount == 2:
        one = jax.random.randint(own_key, (), max(1, total - most), min(most, total - 1) + 1)
        return jnp.stack([one, total - one])
    lengths = jnp.asarray(length_profile(amount, total, most, slope), jnp.int32)
    twos = (amount - 1) // 2
    donor, taker = lengths[1:1 + 2 * twos:2], lengths[2:2 + 2 * twos:2]
    room = jnp.minimum(donor - 1, most - taker)
    shifted = jax.random.randint(jax.random.fold_in(own_key, 1), (twos,), 0, 1 << 20) % (room + 1)
    lengths = lengths.at[1:1 + 2 * twos:2].set(donor - shifted).at[2:2 + 2 * twos:2].set(taker + shifted)
    return lengths[jax.random.permutation(jax.random.fold_in(own_key, 2), amount)]


def gaussian(key, dims, scale, limit, pieces=(), held_as=jnp.bfloat16):
    drawn = jax.random.normal(key, dims, jnp.float32) * scale
    if len(pieces) > 0:
        drawn = block_levels(key, dims, pieces, -0.22, 0.18) * drawn
    return jnp.clip(drawn, min=-limit, max=limit).astype(held_as)


def setup_inputs(seed: int = 0) -> dict:
    splits = jax.random.split(jax.random.key(seed), 6)
    queries = draw_queries(jax.random.fold_in(splits[5], 71), 0)
    key_rows = draw_key_rows(jax.random.fold_in(splits[5], 71), 0)
    value_rows = gaussian(splits[2], (TOKENS, KVH, HD), 1.0, 6.0, ((0, 256),))
    out_grad = gaussian(splits[3], (TOKENS, QH, HD), 1.0, 6.0, ((0, 256),))
    doc_ids = jnp.searchsorted(jnp.cumsum(ragged_sizes(splits[4], DOCS, TOKENS, MOST, 2)), jnp.arange(TOKENS), side="right").astype(jnp.int32)
    return dict(queries=queries, key_rows=key_rows, value_rows=value_rows, out_grad=out_grad, doc_ids=doc_ids)


def reference(queries, key_rows, value_rows, out_grad, doc_ids):
    tok = TOK_DEV
    back = REACH * TOK_DEV
    span = (REACH + 1) * TOK_DEV
    group = QH // KVH
    scale = HD ** -0.5
    pad_k = jnp.concatenate([jnp.zeros((back, KVH, HD), jnp.bfloat16), key_rows], axis=0)
    pad_v = jnp.concatenate([jnp.zeros((back, KVH, HD), jnp.bfloat16), value_rows], axis=0)
    pad_ids = jnp.concatenate([jnp.full((back,), -1, jnp.int32), doc_ids.astype(jnp.int32)], axis=0)
    blocks = TOKENS // tok
    rows = jnp.arange(tok, dtype=jnp.int32)[:, None]
    cols = jnp.arange(span, dtype=jnp.int32)[None, :]

    def step(carry, index):
        acc_k, acc_v = carry
        start = (index * tok).astype(jnp.int32)
        q_blk = lax.dynamic_slice_in_dim(queries, start, tok, 0).astype(jnp.float32).reshape(tok, KVH, group, HD)
        g_blk = lax.dynamic_slice_in_dim(out_grad, start, tok, 0).astype(jnp.float32).reshape(tok, KVH, group, HD)
        k_win = lax.dynamic_slice_in_dim(pad_k, start, span, 0).astype(jnp.float32)
        v_win = lax.dynamic_slice_in_dim(pad_v, start, span, 0).astype(jnp.float32)
        k_ids = lax.dynamic_slice_in_dim(pad_ids, start, span, 0)
        q_ids = lax.dynamic_slice_in_dim(doc_ids.astype(jnp.int32), start, tok, 0)
        allowed = (q_ids[:, None] == k_ids[None, :]) & (cols - back <= rows)
        scores = jnp.einsum("tkgd,ukd->kgtu", q_blk, k_win) * scale
        scores = jnp.where(allowed, scores, -1e30)
        peak = jnp.max(scores, axis=-1, keepdims=True)
        weights = jnp.where(allowed, jnp.exp(scores - peak), 0.0)
        probs = weights / jnp.sum(weights, axis=-1, keepdims=True)
        dprobs = jnp.einsum("tkgd,ukd->kgtu", g_blk, v_win)
        center = jnp.sum(probs * dprobs, axis=-1, keepdims=True)
        dscore = lax.optimization_barrier((probs * (dprobs - center) * scale).astype(jnp.bfloat16)).astype(jnp.float32)
        probs_low = lax.optimization_barrier(probs.astype(jnp.bfloat16)).astype(jnp.float32)
        q_grad = jnp.einsum("kgtu,ukd->tkgd", dscore, k_win).reshape(tok, QH, HD).astype(jnp.bfloat16)
        k_part = jnp.einsum("kgtu,tkgd->ukd", dscore, q_blk)
        v_part = jnp.einsum("kgtu,tkgd->ukd", probs_low, g_blk)
        acc_k = lax.dynamic_update_slice_in_dim(acc_k, lax.dynamic_slice_in_dim(acc_k, start, span, 0) + k_part, start, 0)
        acc_v = lax.dynamic_update_slice_in_dim(acc_v, lax.dynamic_slice_in_dim(acc_v, start, span, 0) + v_part, start, 0)
        return (acc_k, acc_v), q_grad

    empty = jnp.zeros((TOKENS + back, KVH, HD), jnp.float32)
    (acc_k, acc_v), q_parts = lax.scan(step, (empty, empty), jnp.arange(blocks, dtype=jnp.int32))
    query_grad = q_parts.reshape(TOKENS, QH, HD)
    return query_grad, acc_k[back:].astype(jnp.bfloat16), acc_v[back:].astype(jnp.bfloat16)
```

```python
import functools

import jax
import jax.numpy as jnp
from jax import lax
from jax.experimental import pallas as pl
from jax.experimental.pallas import tpu as pltpu
from jax.sharding import PartitionSpec as P

MESH = pl.DeviceIdType.MESH
F32 = jnp.float32
BF16 = jnp.bfloat16
AXES = ("grp", "ctx")
LOG2E = 1.4426950408889634
BLOCKED = -1e30


def contract(a, b, a_dim, b_dim):
    return lax.dot_general(a, b, (((a_dim,), (b_dim,)), ((), ())), preferred_element_type=F32)


def kernel(
    grps, ctxs, group, scale,
    q_hbm, g_hbm, k_rows, v_rows, ids,
    dq, dk_rows, dv_rows,
    q_all, g_all, rows32, near, ids_in, bias, keep,
    acc_k, acc_v, own_sum, tx, rx,
    q_sem, g_sem, send_near, recv_near, send_ids, recv_ids, send_part, recv_part,
):
    tok = q_all.shape[1]
    kvs = near.shape[1]
    count = grps * ctxs
    me = lax.axis_index("grp") * ctxs + lax.axis_index("ctx")

    def at(offset):
        other = lax.rem(me + (offset + count), count)
        return (other // ctxs, lax.rem(other, ctxs))

    barrier = pltpu.get_barrier_semaphore()
    for offset in (1, -1, 3, -3):
        pl.semaphore_signal(barrier, inc=1, device_id=at(offset), device_id_type=MESH)

    def load(c):
        heads = pl.ds(c * group, group)
        return (
            pltpu.make_async_copy(q_hbm.at[heads], q_all.at[heads], q_sem.at[c]),
            pltpu.make_async_copy(g_hbm.at[heads], g_all.at[heads], g_sem.at[c]),
        )

    for c in range(kvs):
        for copy in load(c):
            copy.start()

    for which, rows in ((0, k_rows), (1, v_rows)):
        rows32[which] = rows[...].astype(F32)
        for c in range(kvs):
            near[0, c, which] = rows32[which, pl.ds(c, tok, stride=kvs), :].astype(BF16)
    ids_in[0] = ids[...]

    pl.semaphore_wait(barrier, 4)

    def remote(src, dst, send, recv, offset):
        return pltpu.make_async_remote_copy(
            src_ref=src, dst_ref=dst, send_sem=send, recv_sem=recv,
            device_id=at(offset), device_id_type=MESH,
        )

    def ids_to(slot, source, offset):
        return remote(ids_in.at[source], ids_in.at[slot], send_ids.at[slot], recv_ids.at[slot], offset)

    def direct(c, slot):
        return remote(near.at[0, c], near.at[slot, c], send_near.at[slot, c], recv_near.at[slot, c], slot)

    def relayed(c, which):
        source, offset = ((1, 1), (3, -1))[which]
        slot = (0, 2)[which]
        return remote(
            near.at[source, c, which], near.at[2, c, which],
            send_near.at[slot, c], recv_near.at[slot, c], offset,
        )

    def part(c, kind):
        offset = (-1, 1, -1, -1, -3, -3)[kind]
        return remote(tx.at[c, kind], rx.at[c, kind], send_part.at[kind, c], recv_part.at[kind, c], offset)

    ids_to(1, 0, 1).start()
    ids_to(3, 0, 3).start()
    for c in range(kvs):
        direct(c, 1).start()
        direct(c, 3).start()
    ids_to(1, 0, 1).wait_recv()
    ids_to(2, 1, 1).start()

    def relay(c):
        direct(c, 1).wait_recv()
        relayed(c, 0).start()
        direct(c, 3).wait_recv()
        relayed(c, 1).start()

    relay(0)

    rows_at = lax.broadcasted_iota(jnp.int32, (tok, tok), 0)
    cols_at = lax.broadcasted_iota(jnp.int32, (tok, tok), 1)
    keep[0] = jnp.where(cols_at <= rows_at, 1.0, 0.0).astype(BF16)
    keep[1] = jnp.where(cols_at <= rows_at, 0.0, 1.0).astype(BF16)
    ids_to(3, 0, 3).wait_recv()
    ids_to(2, 1, 1).wait_recv()
    q_ids = jnp.transpose(jnp.broadcast_to(ids_in[0].astype(F32), (tok, tok)))

    def bias_of(slot):
        return jnp.where(jnp.broadcast_to(ids_in[slot].astype(F32), (tok, tok)) == q_ids, 0.0, BLOCKED)

    bias[0] = jnp.where(cols_at <= rows_at, bias_of(0), bias_of(3))
    bias[1] = bias_of(1)
    bias[2] = bias_of(2)

    def one_head(c, i):
        h = c * group + i
        q = q_all[h]
        g = g_all[h]
        lower = lax.broadcasted_iota(jnp.int32, (tok, tok), 1) <= lax.broadcasted_iota(jnp.int32, (tok, tok), 0)
        s = [contract(q, near[o, c, 0], 1, 1) for o in range(4)]
        s = [jnp.where(lower, s[0], s[3]), s[1], s[2]]
        s = [s[o] * (scale * LOG2E) + bias[o] for o in range(3)]
        peak = jnp.max(jnp.maximum(jnp.maximum(s[0], s[1]), s[2]), axis=1, keepdims=True)
        p = [jnp.exp2(x - peak) for x in s]
        inverse = 1.0 / jnp.sum(p[0] + p[1] + p[2], axis=1, keepdims=True)
        d = [contract(g, near[o, c, 1], 1, 1) for o in range(4)]
        d = [jnp.where(lower, d[0], d[3]), d[1], d[2]]
        p = [x * inverse for x in p]
        center = jnp.sum(p[0] * d[0] + p[1] * d[1] + p[2] * d[2], axis=1, keepdims=True)
        ds = [(p[o] * (d[o] - center)).astype(BF16) for o in range(3)]
        p = [x.astype(BF16) for x in p]
        ds = [ds[0] * keep[0], ds[1], ds[2], ds[0] * keep[1]]
        p = [p[0] * keep[0], p[1], p[2], p[0] * keep[1]]
        total = contract(ds[0], near[0, c, 0], 1, 0)
        for o in range(1, 4):
            total = total + contract(ds[o], near[o, c, 0], 1, 0)
        dq[h] = (total * scale).astype(BF16)
        q_turned = jnp.transpose(q.astype(F32)).astype(BF16)
        g_turned = jnp.transpose(g.astype(F32)).astype(BF16)
        for o in range(4):
            dk = contract(q_turned, ds[o], 1, 0)
            dv = contract(g_turned, p[o], 1, 0)
            if i == 0:
                acc_k[o] = dk
                acc_v[o] = dv
            else:
                acc_k[o] += dk
                acc_v[o] += dv

    def middle(c):
        part(c, 0).wait_recv()
        tx[c, 2] = (own_sum[c, 2] + rx[c, 0].astype(F32)).astype(BF16)
        part(c, 2).start()
        part(c, 1).wait_recv()
        tx[c, 5] = (own_sum[c, 3] + rx[c, 1].astype(F32)).astype(BF16)
        part(c, 5).start()

    def finish(c):
        for kind in (3, 4, 2, 5):
            part(c, kind).wait_recv()
        rows32[0, pl.ds(c, tok, stride=kvs), :] = own_sum[c, 0] + (rx[c, 2].astype(F32) + rx[c, 4].astype(F32))
        rows32[1, pl.ds(c, tok, stride=kvs), :] = own_sum[c, 1] + (rx[c, 3].astype(F32) + rx[c, 5].astype(F32))

    def chunk(c, carry):
        relayed(c, 0).wait_recv()
        relayed(c, 1).wait_recv()
        for copy in load(c):
            copy.wait()
        for i in range(group):
            if i == group // 2:
                pl.when(c < kvs - 1)(lambda: relay(c + 1))
                pl.when(c > 0)(lambda: middle(c - 1))
            one_head(c, i)
        tx[c, 0] = (jnp.transpose(acc_k[2]) * scale).astype(BF16)
        part(c, 0).start()
        tx[c, 1] = jnp.transpose(acc_v[2]).astype(BF16)
        part(c, 1).start()
        tx[c, 3] = jnp.transpose(acc_v[1]).astype(BF16)
        part(c, 3).start()
        tx[c, 4] = (jnp.transpose(acc_k[3]) * scale).astype(BF16)
        part(c, 4).start()
        own_sum[c, 2] = jnp.transpose(acc_k[1]) * scale
        own_sum[c, 3] = jnp.transpose(acc_v[3])
        own_sum[c, 0] = jnp.transpose(acc_k[0]) * scale
        own_sum[c, 1] = jnp.transpose(acc_v[0])
        return carry

    lax.fori_loop(0, kvs, chunk, 0)
    middle(kvs - 1)

    def wrap_up(c, carry):
        finish(c)
        direct(c, 1).wait_send()
        direct(c, 3).wait_send()
        relayed(c, 0).wait_send()
        relayed(c, 1).wait_send()
        for kind in range(6):
            part(c, kind).wait_send()
        return carry

    lax.fori_loop(0, kvs, wrap_up, 0)
    ids_to(1, 0, 1).wait_send()
    ids_to(3, 0, 3).wait_send()
    ids_to(2, 1, 1).wait_send()
    dk_rows[...] = rows32[0].astype(BF16)
    dv_rows[...] = rows32[1].astype(BF16)


def shards(grps, ctxs, queries, key_rows, value_rows, out_grad, doc_ids):
    tok, heads, width = queries.shape
    kvs = key_rows.shape[1]
    vmem = pl.BlockSpec(memory_space=pltpu.VMEM)
    anywhere = pl.BlockSpec(memory_space=pl.ANY)
    dma = pltpu.SemaphoreType.DMA
    dq, dk, dv = pl.pallas_call(
        functools.partial(kernel, grps, ctxs, heads // kvs, width ** -0.5),
        out_shape=(
            jax.ShapeDtypeStruct((heads, tok, width), BF16),
            jax.ShapeDtypeStruct((tok * kvs, width), BF16),
            jax.ShapeDtypeStruct((tok * kvs, width), BF16),
        ),
        in_specs=[anywhere, anywhere, vmem, vmem, vmem],
        out_specs=[vmem, vmem, vmem],
        scratch_shapes=[
            pltpu.VMEM((heads, tok, width), BF16),
            pltpu.VMEM((heads, tok, width), BF16),
            pltpu.VMEM((2, tok * kvs, width), F32),
            pltpu.VMEM((4, kvs, 2, tok, width), BF16),
            pltpu.VMEM((4, 1, tok), jnp.int32),
            pltpu.VMEM((3, tok, tok), F32),
            pltpu.VMEM((2, tok, tok), BF16),
            pltpu.VMEM((4, width, tok), F32),
            pltpu.VMEM((4, width, tok), F32),
            pltpu.VMEM((kvs, 4, tok, width), F32),
            pltpu.VMEM((kvs, 6, tok, width), BF16),
            pltpu.VMEM((kvs, 6, tok, width), BF16),
            dma((kvs,)), dma((kvs,)),
            dma((4, kvs)), dma((4, kvs)),
            dma((4,)), dma((4,)),
            dma((6, kvs)), dma((6, kvs)),
        ],
        compiler_params=pltpu.CompilerParams(
            collective_id=0, has_side_effects=True, vmem_limit_bytes=56 * 2**20
        ),
    )(
        jnp.transpose(queries, (1, 0, 2)),
        jnp.transpose(out_grad, (1, 0, 2)),
        key_rows.reshape(tok * kvs, width),
        value_rows.reshape(tok * kvs, width),
        doc_ids.reshape(1, tok),
    )
    return (
        jnp.transpose(dq, (1, 0, 2)),
        dk.reshape(tok, kvs, width),
        dv.reshape(tok, kvs, width),
    )


def solution(mesh):
    spec = P(AXES, None, None)
    return jax.shard_map(
        functools.partial(shards, mesh.shape["grp"], mesh.shape["ctx"]),
        mesh=mesh,
        in_specs=(spec, spec, spec, spec, P(AXES)),
        out_specs=(spec, spec, spec),
        check_vma=False,
    )
```

```python
import functools

import jax
import jax.numpy as jnp
from jax import lax
from jax.experimental import pallas as pl
from jax.experimental.pallas import tpu as pltpu
from jax.sharding import PartitionSpec as P

MESH = pl.DeviceIdType.MESH
F32 = jnp.float32
BF16 = jnp.bfloat16
AXES = ("grp", "ctx")
LOG2E = 1.4426950408889634
BLOCKED = -1e30
RING = 4


def contract(a, b, a_dim, b_dim):
    return lax.dot_general(a, b, (((a_dim,), (b_dim,)), ((), ())), preferred_element_type=F32)


def kernel(
    grps, ctxs, group, scale,
    q_hbm, g_hbm, k_rows, v_rows, ids,
    dq, dk_rows, dv_rows,
    q_all, g_all, rows32, near, ids_in, hot, blocked,
    s_a, s_b, d_a, d_b, ds_all, p_all, q_turned, g_turned, inv_all,
    passing, own_sum, tx, rx,
    q_sem, g_sem, send_near, recv_near, send_ids, recv_ids, send_part, recv_part,
):
    tok = q_all.shape[1]
    kvs = near.shape[0]
    half = tok // 2
    width = q_all.shape[2]
    count = grps * ctxs
    me = lax.axis_index("grp") * ctxs + lax.axis_index("ctx")
    place = lax.rem(me, RING)

    def at(offset):
        other = lax.rem(me + (offset + count), count)
        return (other // ctxs, lax.rem(other, ctxs))

    barrier = pltpu.get_barrier_semaphore()
    for offset in (1, -1, 3, -3, RING, -RING):
        pl.semaphore_signal(barrier, inc=1, device_id=at(offset), device_id_type=MESH)

    def load(c):
        heads = pl.ds(c * group, group)
        return (
            pltpu.make_async_copy(q_hbm.at[heads], q_all.at[heads], q_sem.at[c]),
            pltpu.make_async_copy(g_hbm.at[heads], g_all.at[heads], g_sem.at[c]),
        )

    for c in range(kvs):
        for copy in load(c):
            copy.start()

    def block(slot):
        return pl.ds(slot * tok, tok)

    for which, rows in ((0, k_rows), (1, v_rows)):
        rows32[which] = rows[...].astype(F32)
        for c in range(kvs):
            near[c, which, block(0)] = rows32[which, pl.ds(c, tok, stride=kvs), :].astype(BF16)
    ids_in[0] = ids[...]

    pl.semaphore_wait(barrier, 6)

    def remote(src, dst, send, recv, offset):
        return pltpu.make_async_remote_copy(
            src_ref=src, dst_ref=dst, send_sem=send, recv_sem=recv,
            device_id=at(offset), device_id_type=MESH,
        )

    def ids_to(slot, source, offset):
        return remote(ids_in.at[source], ids_in.at[slot], send_ids.at[slot], recv_ids.at[slot], offset)

    moves = ((0, 0, 1, 1), (0, 0, 3, 3), (1, 0, 3, 3), (1, 0, 1, 1), (0, 1, 2, 1), (1, 3, 2, -1))

    def move(c, kind):
        which, source, slot, offset = moves[kind]
        return remote(
            near.at[c, which, block(source)], near.at[c, which, block(slot)],
            send_near.at[kind, c], recv_near.at[kind, c], offset,
        )

    def onward(c, which):
        return remote(
            near.at[c, which, block(0)], passing.at[c, which],
            send_near.at[6 + which, c], recv_near.at[6 + which, c], RING,
        )

    def handed(c, kind):
        which, _, slot, offset = moves[kind]
        return remote(
            passing.at[c, which], near.at[c, which, block(slot)],
            send_near.at[kind, c], recv_near.at[kind, c], offset - RING,
        )

    def feed(c):
        @pl.when(place == RING - 1)
        def _():
            for which in range(2):
                onward(c, which).start()

        @pl.when(place != RING - 1)
        def _():
            for kind in range(4):
                move(c, kind).start()

    def forward(c):
        @pl.when(place == RING - 1)
        def _():
            onward(c, 0).wait_recv()
            handed(c, 0).start()
            handed(c, 1).start()
            onward(c, 1).wait_recv()
            handed(c, 2).start()
            handed(c, 3).start()

    def relay(c):
        move(c, 0).wait_recv()
        move(c, 4).start()
        move(c, 2).wait_recv()
        move(c, 5).start()

    def part(c, kind, shift=0):
        offset = (-1, 1, -1, -1, -3, -3, -RING, -RING)[kind] + shift
        return remote(tx.at[c, kind], rx.at[c, kind], send_part.at[kind, c], recv_part.at[kind, c], offset)

    def give(c, kind):
        turn = (0, 0, 0, 0, 2, 2)[kind]

        @pl.when(place == turn)
        def _():
            part(c, kind, RING).start()

        @pl.when(place != turn)
        def _():
            part(c, kind).start()

    def join(c):
        @pl.when(place == RING - 1)
        def _():
            for kind in (2, 4):
                part(c, kind).wait_recv()
            tx[c, 6] = (rx[c, 2].astype(F32) + rx[c, 4].astype(F32)).astype(BF16)
            part(c, 6).start()
            for kind in (3, 5):
                part(c, kind).wait_recv()
            tx[c, 7] = (rx[c, 3].astype(F32) + rx[c, 5].astype(F32)).astype(BF16)
            part(c, 7).start()

    ids_to(1, 0, 1).start()
    ids_to(3, 0, 3).start()
    feed(0)
    ids_to(1, 0, 1).wait_recv()
    ids_to(2, 1, 1).start()
    forward(0)
    feed(1)
    relay(0)
    forward(1)
    feed(2)

    lanes = lax.broadcasted_iota(jnp.int32, (tok, width), 1).astype(F32)

    def column(slot):
        return jnp.transpose(jnp.broadcast_to(ids_in[slot].astype(F32), (width, tok)))

    hot[...] = jnp.where(column(0) == lanes, 1.0, 0.0).astype(BF16)
    ids_to(3, 0, 3).wait_recv()
    ids_to(2, 1, 1).wait_recv()
    for slot in range(4):
        blocked[block(slot)] = jnp.where(column(slot) == lanes, 0.0, BLOCKED).astype(BF16)
    low = lax.broadcasted_iota(jnp.int32, (half, half), 1) <= lax.broadcasted_iota(jnp.int32, (half, half), 0)
    keep = [jnp.where(low, 1.0, 0.0).astype(BF16), jnp.where(low, 0.0, 1.0).astype(BF16)]

    def corners(ref):
        for i in range(group):
            ref[i * tok:i * tok + half, half:tok] = jnp.zeros((half, half), BF16)
            ref[i * tok + half:(i + 1) * tok, 3 * tok:3 * tok + half] = jnp.zeros((half, half), BF16)

    corners(p_all)
    for c in range(kvs):
        corners(ds_all.at[c])

    def products(c, h, slot, step):
        q = jnp.concatenate([q_all[h], hot[...]], axis=1)
        g = g_all[h]
        for out, rows, right in (
            ((s_a, s_b)[slot], q, lambda o: jnp.concatenate([near[c, 0, block(o)], blocked[block(o)]], axis=1)),
            ((d_a, d_b)[slot], g, lambda o: near[c, 1, block(o)]),
        ):
            if step in (1, 2):
                out[:, step * tok:(step + 1) * tok] = contract(rows, right(step), 1, 1)
            if step == 0:
                own = contract(rows, right(0), 1, 1)
                third = contract(rows, right(3), 1, 1)
                out[:half, :half] = jnp.where(low, own[:half, :half], third[:half, :half])
                out[:half, half:tok] = third[:half, half:]
                out[half:, :half] = own[half:, :half]
                out[half:, half:tok] = jnp.where(low, own[half:, half:], third[half:, half:])

    steps = 8
    some = tok // steps

    def spread(ref, i, first, x):
        rows = slice(i * tok + first, i * tok + first + some)
        part_of = slice(first % half, first % half + some)
        ref[rows, tok:3 * tok] = x[:, tok:]
        if first < half:
            ref[rows, :half] = x[:, :half] * keep[0][part_of]
            ref[rows, 3 * tok:3 * tok + half] = x[:, :half] * keep[1][part_of]
            ref[rows, 3 * tok + half:] = x[:, half:tok]
        else:
            ref[rows, :half] = x[:, :half]
            ref[rows, half:tok] = x[:, half:tok] * keep[0][part_of]
            ref[rows, 3 * tok + half:] = x[:, half:tok] * keep[1][part_of]

    def softmax(c, h, i, step):
        first = step * some
        rows = slice(first, first + some)
        s = (s_a, s_b)[i % 2][rows]
        d = (d_a, d_b)[i % 2][rows]
        peak = jnp.max(s, axis=1, keepdims=True)
        p = jnp.exp2((s - peak) * (scale * LOG2E))
        inverse = 1.0 / jnp.sum(p, axis=1, keepdims=True)
        center = jnp.sum(p * d, axis=1, keepdims=True) * inverse
        spread(ds_all.at[c], i, first, (p * (d - center)).astype(BF16))
        spread(p_all, i, first, p.astype(BF16))
        inv_all[c, i * tok + first:i * tok + first + some] = jnp.broadcast_to(inverse, (some, width))
        if step == steps - 1:
            head = slice(i * tok, (i + 1) * tok)
            q_turned[:, head] = jnp.transpose(q_all[h].astype(F32) * inv_all[c, head]).astype(BF16)
            g_turned[:, head] = jnp.transpose(g_all[h].astype(F32) * inv_all[c, head]).astype(BF16)

    def query_part(c, h, i):
        head = slice(i * tok, (i + 1) * tok)
        dq[h] = (contract(ds_all[c, head], near[c, 0], 1, 0) * (inv_all[c, head] * scale)).astype(BF16)

    def key_part(c, slot):
        x = contract(q_turned[...], ds_all[c, :, slot * tok:(slot + 1) * tok], 1, 0)
        return jnp.transpose(x) * scale

    def value_part(slot):
        x = contract(g_turned[...], p_all[:, slot * tok:(slot + 1) * tok], 1, 0)
        return jnp.transpose(x)

    def interleave(*items):
        for step in range(steps):
            for work, args, number in items:
                for one in range(step * number // steps, (step + 1) * number // steps):
                    work(*args, one)

    def middle(c):
        part(c, 0).wait_recv()
        tx[c, 2] = (own_sum[c, 2] + rx[c, 0].astype(F32)).astype(BF16)
        give(c, 2)
        part(c, 1).wait_recv()
        tx[c, 5] = (own_sum[c, 3] + rx[c, 1].astype(F32)).astype(BF16)
        give(c, 5)

    def finish(c):
        def total(which, kinds):
            for kind in kinds:
                part(c, kind).wait_recv()
            x = rx[c, kinds[0]].astype(F32)
            for kind in kinds[1:]:
                x = x + rx[c, kind].astype(F32)
            rows32[which, pl.ds(c, tok, stride=kvs), :] = own_sum[c, which] + x

        @pl.when(place == RING - 1)
        def _():
            total(0, (6,))
            total(1, (7,))

        @pl.when(place != RING - 1)
        def _():
            total(0, (2, 4))
            total(1, (3, 5))

    def chunk(c, carry):
        for kind in (1, 3, 4, 5):
            move(c, kind).wait_recv()
        for copy in load(c):
            copy.wait()

        def first(i):
            return (products, (c, c * group + i, i % 2), 4)

        def second(i):
            return (softmax, (c, c * group + i, i), steps)

        events = ((3, 1, relay), (5, 2, forward), (5, 3, feed), (4, -2, join), (6, -1, middle))
        interleave(first(0))
        interleave(second(0), first(1))
        for i in range(2, group):
            for when, ahead, event in events:
                if when == i:
                    pl.when((c + ahead >= 0) & (c + ahead < kvs))(functools.partial(event, c + ahead))
            interleave(second(i - 1), first(i))
        interleave(second(group - 1))
        tx[c, 0] = key_part(c, 2).astype(BF16)
        part(c, 0).start()
        tx[c, 1] = value_part(2).astype(BF16)
        part(c, 1).start()
        tx[c, 3] = value_part(1).astype(BF16)
        give(c, 3)
        tx[c, 4] = key_part(c, 3).astype(BF16)
        give(c, 4)
        own_sum[c, 2] = key_part(c, 1)
        own_sum[c, 3] = value_part(3)
        own_sum[c, 0] = key_part(c, 0)
        own_sum[c, 1] = value_part(0)
        return carry

    def queries_of(c, carry):
        for i in range(group):
            query_part(c, c * group + i, i)
        return carry

    lax.fori_loop(0, kvs, chunk, 0)
    lax.fori_loop(0, kvs // 2, queries_of, 0)
    join(kvs - 2)
    middle(kvs - 1)
    join(kvs - 1)
    lax.fori_loop(kvs // 2, kvs, queries_of, 0)

    def wrap_up(c, carry):
        finish(c)
        for kind in range(6):
            move(c, kind).wait_send()
            part(c, kind).wait_send()

        @pl.when(place == RING - 1)
        def _():
            for which in range(2):
                onward(c, which).wait_send()
                part(c, 6 + which).wait_send()

        return carry

    lax.fori_loop(0, kvs, wrap_up, 0)
    ids_to(1, 0, 1).wait_send()
    ids_to(3, 0, 3).wait_send()
    ids_to(2, 1, 1).wait_send()
    dk_rows[...] = rows32[0].astype(BF16)
    dv_rows[...] = rows32[1].astype(BF16)


def shards(grps, ctxs, queries, key_rows, value_rows, out_grad, doc_ids):
    tok, heads, width = queries.shape
    kvs = key_rows.shape[1]
    group = heads // kvs
    vmem = pl.BlockSpec(memory_space=pltpu.VMEM)
    anywhere = pl.BlockSpec(memory_space=pl.ANY)
    dma = pltpu.SemaphoreType.DMA
    dq, dk, dv = pl.pallas_call(
        functools.partial(kernel, grps, ctxs, group, width ** -0.5),
        out_shape=(
            pltpu.VMEM((heads, tok, width), BF16),
            jax.ShapeDtypeStruct((tok * kvs, width), BF16),
            jax.ShapeDtypeStruct((tok * kvs, width), BF16),
        ),
        in_specs=[anywhere, anywhere, vmem, vmem, vmem],
        out_specs=[vmem, vmem, vmem],
        scratch_shapes=[
            pltpu.VMEM((heads, tok, width), BF16),
            pltpu.VMEM((heads, tok, width), BF16),
            pltpu.VMEM((2, tok * kvs, width), F32),
            pltpu.VMEM((kvs, 2, 4 * tok, width), BF16),
            pltpu.VMEM((4, 1, tok), jnp.int32),
            pltpu.VMEM((tok, width), BF16),
            pltpu.VMEM((4 * tok, width), BF16),
            pltpu.VMEM((tok, 3 * tok), F32),
            pltpu.VMEM((tok, 3 * tok), F32),
            pltpu.VMEM((tok, 3 * tok), F32),
            pltpu.VMEM((tok, 3 * tok), F32),
            pltpu.VMEM((kvs, group * tok, 4 * tok), BF16),
            pltpu.VMEM((group * tok, 4 * tok), BF16),
            pltpu.VMEM((width, group * tok), BF16),
            pltpu.VMEM((width, group * tok), BF16),
            pltpu.VMEM((kvs, group * tok, width), F32),
            pltpu.VMEM((kvs, 2, tok, width), BF16),
            pltpu.VMEM((kvs, 4, tok, width), F32),
            pltpu.VMEM((kvs, 8, tok, width), BF16),
            pltpu.VMEM((kvs, 8, tok, width), BF16),
            dma((kvs,)), dma((kvs,)),
            dma((8, kvs)), dma((8, kvs)),
            dma((4,)), dma((4,)),
            dma((8, kvs)), dma((8, kvs)),
        ],
        compiler_params=pltpu.CompilerParams(
            collective_id=0, has_side_effects=True, vmem_limit_bytes=56 * 2**20
        ),
    )(
        jnp.transpose(queries, (1, 0, 2)),
        jnp.transpose(out_grad, (1, 0, 2)),
        key_rows.reshape(tok * kvs, width),
        value_rows.reshape(tok * kvs, width),
        doc_ids.reshape(1, tok),
    )
    return (
        jnp.transpose(dq, (1, 0, 2)),
        dk.reshape(tok, kvs, width),
        dv.reshape(tok, kvs, width),
    )


def solution(mesh):
    spec = P(AXES, None, None)
    return jax.shard_map(
        functools.partial(shards, mesh.shape["grp"], mesh.shape["ctx"]),
        mesh=mesh,
        in_specs=(spec, spec, spec, spec, P(AXES)),
        out_specs=(spec, spec, spec),
        check_vma=False,
    )
```

```python
import functools

import jax
import jax.numpy as jnp
from jax import lax
from jax.experimental import pallas as pl
from jax.experimental.pallas import tpu as pltpu
from jax.sharding import PartitionSpec as P

MESH = pl.DeviceIdType.MESH
F32 = jnp.float32
BF16 = jnp.bfloat16
AXES = ("grp", "ctx")
LOG2E = 1.4426950408889634
BLOCKED = -1e30
RING = 4


def contract(a, b, a_dim, b_dim):
    return lax.dot_general(a, b, (((a_dim,), (b_dim,)), ((), ())), preferred_element_type=F32)


def kernel(
    grps, ctxs, group, scale,
    q_hbm, g_hbm, k_hbm, v_hbm, ids,
    dq, dk_rows, dv_rows,
    q_all, g_all, k_rows, v_rows, rows32, near, ids_in, hot, blocked,
    s_a, s_b, d_a, d_b, ds_all, p_all, q_turned, g_turned, inv_all,
    passing, own_sum, tx, rx,
    q_sem, g_sem, rows_sem, send_near, recv_near, send_ids, recv_ids, send_part, recv_part,
):
    tok = q_all.shape[1]
    kvs = near.shape[0]
    half = tok // 2
    width = q_all.shape[2]
    count = grps * ctxs
    me = lax.axis_index("grp") * ctxs + lax.axis_index("ctx")
    place = lax.rem(me, RING)

    def at(offset):
        other = lax.rem(me + (offset + count), count)
        return (other // ctxs, lax.rem(other, ctxs))

    barrier = pltpu.get_barrier_semaphore()
    for offset in (1, -1, 3, -3, RING, -RING):
        pl.semaphore_signal(barrier, inc=1, device_id=at(offset), device_id_type=MESH)

    def load(c):
        heads = pl.ds(c * group, group)
        return (
            pltpu.make_async_copy(q_hbm.at[heads], q_all.at[heads], q_sem.at[c]),
            pltpu.make_async_copy(g_hbm.at[heads], g_all.at[heads], g_sem.at[c]),
        )

    rows_in = [
        pltpu.make_async_copy(hbm, rows, rows_sem.at[which])
        for which, (hbm, rows) in enumerate(((k_hbm, k_rows), (v_hbm, v_rows)))
    ]
    for copy in rows_in:
        copy.start()
    for c in range(kvs):
        for copy in load(c):
            copy.start()

    def block(slot):
        return pl.ds(slot * tok, tok)

    def split(c):
        for which in range(2):
            near[c, which, block(0)] = rows32[which, pl.ds(c, tok, stride=kvs), :].astype(BF16)

    for which, rows in ((0, k_rows), (1, v_rows)):
        rows_in[which].wait()
        rows32[which] = rows[...].astype(F32)
    split(0)
    ids_in[0] = ids[...]

    pl.semaphore_wait(barrier, 6)

    def remote(src, dst, send, recv, offset):
        return pltpu.make_async_remote_copy(
            src_ref=src, dst_ref=dst, send_sem=send, recv_sem=recv,
            device_id=at(offset), device_id_type=MESH,
        )

    def ids_to(slot, source, offset):
        return remote(ids_in.at[source], ids_in.at[slot], send_ids.at[slot], recv_ids.at[slot], offset)

    moves = ((0, 0, 1, 1), (0, 0, 3, 3), (1, 0, 3, 3), (1, 0, 1, 1), (0, 1, 2, 1), (1, 3, 2, -1))

    def move(c, kind):
        which, source, slot, offset = moves[kind]
        return remote(
            near.at[c, which, block(source)], near.at[c, which, block(slot)],
            send_near.at[kind, c], recv_near.at[kind, c], offset,
        )

    def onward(c, which):
        return remote(
            near.at[c, which, block(0)], passing.at[c, which],
            send_near.at[6 + which, c], recv_near.at[6 + which, c], RING,
        )

    def handed(c, kind):
        which, _, slot, offset = moves[kind]
        return remote(
            passing.at[c, which], near.at[c, which, block(slot)],
            send_near.at[kind, c], recv_near.at[kind, c], offset - RING,
        )

    def feed(c):
        @pl.when(place == RING - 1)
        def _():
            for which in range(2):
                onward(c, which).start()

        @pl.when(place != RING - 1)
        def _():
            for kind in range(4):
                move(c, kind).start()

    def forward(c):
        @pl.when(place == RING - 1)
        def _():
            onward(c, 0).wait_recv()
            handed(c, 0).start()
            handed(c, 1).start()
            onward(c, 1).wait_recv()
            handed(c, 2).start()
            handed(c, 3).start()

    def relay(c):
        move(c, 0).wait_recv()
        move(c, 4).start()
        move(c, 2).wait_recv()
        move(c, 5).start()

    def part(c, kind, shift=0):
        offset = (-1, 1, -1, -1, -3, -3, -RING, -RING)[kind] + shift
        return remote(tx.at[c, kind], rx.at[c, kind], send_part.at[kind, c], recv_part.at[kind, c], offset)

    def give(c, kind):
        turn = (0, 0, 0, 0, 2, 2)[kind]

        @pl.when(place == turn)
        def _():
            part(c, kind, RING).start()

        @pl.when(place != turn)
        def _():
            part(c, kind).start()

    def join(c):
        @pl.when(place == RING - 1)
        def _():
            for kind in (2, 4):
                part(c, kind).wait_recv()
            tx[c, 6] = (rx[c, 2].astype(F32) + rx[c, 4].astype(F32)).astype(BF16)
            part(c, 6).start()
            for kind in (3, 5):
                part(c, kind).wait_recv()
            tx[c, 7] = (rx[c, 3].astype(F32) + rx[c, 5].astype(F32)).astype(BF16)
            part(c, 7).start()

    ids_to(1, 0, 1).start()
    ids_to(3, 0, 3).start()
    feed(0)
    for c in range(1, kvs):
        split(c)
    ids_to(1, 0, 1).wait_recv()
    ids_to(2, 1, 1).start()
    forward(0)
    feed(1)
    relay(0)
    forward(1)
    feed(2)

    lanes = lax.broadcasted_iota(jnp.int32, (tok, width), 1).astype(F32)

    def column(slot):
        return jnp.transpose(jnp.broadcast_to(ids_in[slot].astype(F32), (width, tok)))

    hot[...] = jnp.where(column(0) == lanes, 1.0, 0.0).astype(BF16)
    ids_to(3, 0, 3).wait_recv()
    ids_to(2, 1, 1).wait_recv()
    for slot in range(4):
        blocked[block(slot)] = jnp.where(column(slot) == lanes, 0.0, BLOCKED).astype(BF16)
    low = lax.broadcasted_iota(jnp.int32, (half, half), 1) <= lax.broadcasted_iota(jnp.int32, (half, half), 0)
    keep = [jnp.where(low, 1.0, 0.0).astype(BF16), jnp.where(low, 0.0, 1.0).astype(BF16)]

    def corners(ref):
        for i in range(group):
            ref[i * tok:i * tok + half, half:tok] = jnp.zeros((half, half), BF16)
            ref[i * tok + half:(i + 1) * tok, 3 * tok:3 * tok + half] = jnp.zeros((half, half), BF16)

    corners(p_all)
    for c in range(kvs):
        corners(ds_all.at[c])

    def products(c, h, slot, step):
        q = jnp.concatenate([q_all[h], hot[...]], axis=1)
        g = g_all[h]
        for out, rows, right in (
            ((s_a, s_b)[slot], q, lambda o: jnp.concatenate([near[c, 0, block(o)], blocked[block(o)]], axis=1)),
            ((d_a, d_b)[slot], g, lambda o: near[c, 1, block(o)]),
        ):
            if step in (1, 2):
                out[:, step * tok:(step + 1) * tok] = contract(rows, right(step), 1, 1)
            if step == 0:
                own = contract(rows, right(0), 1, 1)
                third = contract(rows, right(3), 1, 1)
                out[:half, :half] = jnp.where(low, own[:half, :half], third[:half, :half])
                out[:half, half:tok] = third[:half, half:]
                out[half:, :half] = own[half:, :half]
                out[half:, half:tok] = jnp.where(low, own[half:, half:], third[half:, half:])

    steps = 8
    some = tok // steps

    def spread(ref, i, first, x):
        rows = slice(i * tok + first, i * tok + first + some)
        part_of = slice(first % half, first % half + some)
        ref[rows, tok:3 * tok] = x[:, tok:]
        if first < half:
            ref[rows, :half] = x[:, :half] * keep[0][part_of]
            ref[rows, 3 * tok:3 * tok + half] = x[:, :half] * keep[1][part_of]
            ref[rows, 3 * tok + half:] = x[:, half:tok]
        else:
            ref[rows, :half] = x[:, :half]
            ref[rows, half:tok] = x[:, half:tok] * keep[0][part_of]
            ref[rows, 3 * tok + half:] = x[:, half:tok] * keep[1][part_of]

    def softmax(c, h, i, step):
        first = step * some
        rows = slice(first, first + some)
        s = (s_a, s_b)[i % 2][rows]
        d = (d_a, d_b)[i % 2][rows]
        peak = jnp.max(s, axis=1, keepdims=True)
        p = jnp.exp2((s - peak) * (scale * LOG2E))
        inverse = 1.0 / jnp.sum(p, axis=1, keepdims=True)
        center = jnp.sum(p * d, axis=1, keepdims=True) * inverse
        spread(ds_all.at[c], i, first, (p * (d - center)).astype(BF16))
        spread(p_all, i, first, p.astype(BF16))
        inv_all[c, i * tok + first:i * tok + first + some] = jnp.broadcast_to(inverse, (some, width))
        if step == steps - 1:
            head = slice(i * tok, (i + 1) * tok)
            q_turned[:, head] = jnp.transpose(q_all[h].astype(F32) * inv_all[c, head]).astype(BF16)
            g_turned[:, head] = jnp.transpose(g_all[h].astype(F32) * inv_all[c, head]).astype(BF16)

    def query_part(c, h, i):
        head = slice(i * tok, (i + 1) * tok)
        dq[h] = (contract(ds_all[c, head], near[c, 0], 1, 0) * (inv_all[c, head] * scale)).astype(BF16)

    def key_part(c, slot):
        x = contract(q_turned[...], ds_all[c, :, slot * tok:(slot + 1) * tok], 1, 0)
        return jnp.transpose(x) * scale

    def value_part(slot):
        x = contract(g_turned[...], p_all[:, slot * tok:(slot + 1) * tok], 1, 0)
        return jnp.transpose(x)

    def interleave(*items):
        for step in range(steps):
            for work, args, number in items:
                for one in range(step * number // steps, (step + 1) * number // steps):
                    work(*args, one)

    def middle(c):
        part(c, 0).wait_recv()
        tx[c, 2] = (own_sum[c, 2] + rx[c, 0].astype(F32)).astype(BF16)
        give(c, 2)
        part(c, 1).wait_recv()
        tx[c, 5] = (own_sum[c, 3] + rx[c, 1].astype(F32)).astype(BF16)
        give(c, 5)

    def finish(c):
        def total(which, kinds):
            for kind in kinds:
                part(c, kind).wait_recv()
            x = rx[c, kinds[0]].astype(F32)
            for kind in kinds[1:]:
                x = x + rx[c, kind].astype(F32)
            rows32[which, pl.ds(c, tok, stride=kvs), :] = own_sum[c, which] + x

        @pl.when(place == RING - 1)
        def _():
            total(0, (6,))
            total(1, (7,))

        @pl.when(place != RING - 1)
        def _():
            total(0, (2, 4))
            total(1, (3, 5))

    def chunk(c, carry):
        for kind in (1, 3, 4, 5):
            move(c, kind).wait_recv()
        for copy in load(c):
            copy.wait()

        def first(i):
            return (products, (c, c * group + i, i % 2), 4)

        def second(i):
            return (softmax, (c, c * group + i, i), steps)

        events = ((3, 1, relay), (5, 2, forward), (5, 3, feed), (6, -1, middle), (6, -2, join))
        interleave(first(0))
        interleave(second(0), first(1))
        for i in range(2, group):
            for when, ahead, event in events:
                if when == i:
                    pl.when((c + ahead >= 0) & (c + ahead < kvs))(functools.partial(event, c + ahead))
            interleave(second(i - 1), first(i))
        interleave(second(group - 1))
        tx[c, 0] = key_part(c, 2).astype(BF16)
        part(c, 0).start()
        tx[c, 1] = value_part(2).astype(BF16)
        part(c, 1).start()
        tx[c, 3] = value_part(1).astype(BF16)
        give(c, 3)
        tx[c, 4] = key_part(c, 3).astype(BF16)
        give(c, 4)
        own_sum[c, 2] = key_part(c, 1)
        own_sum[c, 3] = value_part(3)
        own_sum[c, 0] = key_part(c, 0)
        own_sum[c, 1] = value_part(0)
        return carry

    def queries_of(c, carry):
        for i in range(group):
            query_part(c, c * group + i, i)
        return carry

    def ended(c, carry):
        finish(c)
        return carry

    lax.fori_loop(0, kvs, chunk, 0)
    join(kvs - 2)
    lax.fori_loop(0, kvs // 4, queries_of, 0)
    middle(kvs - 1)
    lax.fori_loop(kvs // 4, kvs, queries_of, 0)
    lax.fori_loop(0, kvs - 1, ended, 0)
    join(kvs - 1)
    finish(kvs - 1)

    def wrap_up(c, carry):
        for kind in range(6):
            move(c, kind).wait_send()
            part(c, kind).wait_send()

        @pl.when(place == RING - 1)
        def _():
            for which in range(2):
                onward(c, which).wait_send()
                part(c, 6 + which).wait_send()

        return carry

    lax.fori_loop(0, kvs, wrap_up, 0)
    ids_to(1, 0, 1).wait_send()
    ids_to(3, 0, 3).wait_send()
    ids_to(2, 1, 1).wait_send()
    dk_rows[...] = rows32[0].astype(BF16)
    dv_rows[...] = rows32[1].astype(BF16)


def shards(grps, ctxs, queries, key_rows, value_rows, out_grad, doc_ids):
    tok, heads, width = queries.shape
    kvs = key_rows.shape[1]
    group = heads // kvs
    vmem = pl.BlockSpec(memory_space=pltpu.VMEM)
    anywhere = pl.BlockSpec(memory_space=pl.ANY)
    dma = pltpu.SemaphoreType.DMA
    dq, dk, dv = pl.pallas_call(
        functools.partial(kernel, grps, ctxs, group, width ** -0.5),
        out_shape=(
            pltpu.VMEM((heads, tok, width), BF16),
            pltpu.VMEM((tok * kvs, width), BF16),
            pltpu.VMEM((tok * kvs, width), BF16),
        ),
        in_specs=[anywhere, anywhere, anywhere, anywhere, vmem],
        out_specs=[vmem, vmem, vmem],
        scratch_shapes=[
            pltpu.VMEM((heads, tok, width), BF16),
            pltpu.VMEM((heads, tok, width), BF16),
            pltpu.VMEM((tok * kvs, width), BF16),
            pltpu.VMEM((tok * kvs, width), BF16),
            pltpu.VMEM((2, tok * kvs, width), F32),
            pltpu.VMEM((kvs, 2, 4 * tok, width), BF16),
            pltpu.VMEM((4, 1, tok), jnp.int32),
            pltpu.VMEM((tok, width), BF16),
            pltpu.VMEM((4 * tok, width), BF16),
            pltpu.VMEM((tok, 3 * tok), F32),
            pltpu.VMEM((tok, 3 * tok), F32),
            pltpu.VMEM((tok, 3 * tok), F32),
            pltpu.VMEM((tok, 3 * tok), F32),
            pltpu.VMEM((kvs, group * tok, 4 * tok), BF16),
            pltpu.VMEM((group * tok, 4 * tok), BF16),
            pltpu.VMEM((width, group * tok), BF16),
            pltpu.VMEM((width, group * tok), BF16),
            pltpu.VMEM((kvs, group * tok, width), F32),
            pltpu.VMEM((kvs, 2, tok, width), BF16),
            pltpu.VMEM((kvs, 4, tok, width), F32),
            pltpu.VMEM((kvs, 8, tok, width), BF16),
            pltpu.VMEM((kvs, 8, tok, width), BF16),
            dma((kvs,)), dma((kvs,)), dma((2,)),
            dma((8, kvs)), dma((8, kvs)),
            dma((4,)), dma((4,)),
            dma((8, kvs)), dma((8, kvs)),
        ],
        compiler_params=pltpu.CompilerParams(
            collective_id=0, has_side_effects=True, vmem_limit_bytes=56 * 2**20
        ),
    )(
        jnp.transpose(queries, (1, 0, 2)),
        jnp.transpose(out_grad, (1, 0, 2)),
        key_rows.reshape(tok * kvs, width),
        value_rows.reshape(tok * kvs, width),
        doc_ids.reshape(1, tok),
    )
    return (
        jnp.transpose(dq, (1, 0, 2)),
        dk.reshape(tok, kvs, width),
        dv.reshape(tok, kvs, width),
    )


def solution(mesh):
    spec = P(AXES, None, None)
    return jax.shard_map(
        functools.partial(shards, mesh.shape["grp"], mesh.shape["ctx"]),
        mesh=mesh,
        in_specs=(spec, spec, spec, spec, P(AXES)),
        out_specs=(spec, spec, spec),
        check_vma=False,
    )
```

```python
import functools

import jax
import jax.numpy as jnp
from jax import lax
from jax.experimental import pallas as pl
from jax.experimental.pallas import tpu as pltpu
from jax.sharding import PartitionSpec as P

MESH = pl.DeviceIdType.MESH
F32 = jnp.float32
BF16 = jnp.bfloat16
AXES = ("grp", "ctx")
LOG2E = 1.4426950408889634
BLOCKED = -1e30
RING = 4


def contract(a, b, a_dim, b_dim):
    return lax.dot_general(a, b, (((a_dim,), (b_dim,)), ((), ())), preferred_element_type=F32)


def kernel(
    grps, ctxs, group, scale,
    q_hbm, g_hbm, k_hbm, v_hbm, ids,
    dq, dk_rows, dv_rows,
    q_all, g_all, k_rows, v_rows, rows32, near, ids_in, hot, blocked,
    s_a, s_b, d_a, d_b, ds_all, p_all, q_turned, g_turned, inv_all,
    passing, own_sum, tx, rx,
    q_sem, g_sem, rows_sem, send_near, recv_near, send_ids, recv_ids, send_part, recv_part,
):
    tok = q_all.shape[1]
    kvs = near.shape[0]
    half = tok // 2
    width = q_all.shape[2]
    count = grps * ctxs
    me = lax.axis_index("grp") * ctxs + lax.axis_index("ctx")
    place = lax.rem(me, RING)

    def at(offset):
        other = lax.rem(me + (offset + count), count)
        return (other // ctxs, lax.rem(other, ctxs))

    barrier = pltpu.get_barrier_semaphore()
    for offset in (1, -1, 3, -3, RING, -RING):
        pl.semaphore_signal(barrier, inc=1, device_id=at(offset), device_id_type=MESH)

    def load(c):
        heads = pl.ds(c * group, group)
        return (
            pltpu.make_async_copy(q_hbm.at[heads], q_all.at[heads], q_sem.at[c]),
            pltpu.make_async_copy(g_hbm.at[heads], g_all.at[heads], g_sem.at[c]),
        )

    rows_in = [
        pltpu.make_async_copy(hbm, rows, rows_sem.at[which])
        for which, (hbm, rows) in enumerate(((k_hbm, k_rows), (v_hbm, v_rows)))
    ]
    for copy in rows_in:
        copy.start()
    for c in range(kvs):
        for copy in load(c):
            copy.start()

    def block(slot):
        return pl.ds(slot * tok, tok)

    def split(c):
        for which in range(2):
            near[c, which, block(0)] = rows32[which, pl.ds(c, tok, stride=kvs), :].astype(BF16)

    for which, rows in ((0, k_rows), (1, v_rows)):
        rows_in[which].wait()
        rows32[which] = rows[...].astype(F32)
    split(0)
    ids_in[0] = ids[...]

    pl.semaphore_wait(barrier, 6)

    def remote(src, dst, send, recv, offset):
        return pltpu.make_async_remote_copy(
            src_ref=src, dst_ref=dst, send_sem=send, recv_sem=recv,
            device_id=at(offset), device_id_type=MESH,
        )

    def ids_to(slot, source, offset):
        return remote(ids_in.at[source], ids_in.at[slot], send_ids.at[slot], recv_ids.at[slot], offset)

    moves = ((0, 0, 1, 1), (0, 0, 3, 3), (1, 0, 3, 3), (1, 0, 1, 1), (0, 1, 2, 1), (1, 3, 2, -1))

    def move(c, kind):
        which, source, slot, offset = moves[kind]
        return remote(
            near.at[c, which, block(source)], near.at[c, which, block(slot)],
            send_near.at[kind, c], recv_near.at[kind, c], offset,
        )

    def onward(c, which):
        return remote(
            near.at[c, which, block(0)], passing.at[c, which],
            send_near.at[6 + which, c], recv_near.at[6 + which, c], RING,
        )

    def handed(c, kind):
        which, _, slot, offset = moves[kind]
        return remote(
            passing.at[c, which], near.at[c, which, block(slot)],
            send_near.at[kind, c], recv_near.at[kind, c], offset - RING,
        )

    def feed(c):
        @pl.when(place == RING - 1)
        def _():
            for which in range(2):
                onward(c, which).start()

        @pl.when(place != RING - 1)
        def _():
            for kind in range(4):
                move(c, kind).start()

    def forward(c):
        @pl.when(place == RING - 1)
        def _():
            onward(c, 0).wait_recv()
            handed(c, 0).start()
            handed(c, 1).start()
            onward(c, 1).wait_recv()
            handed(c, 2).start()
            handed(c, 3).start()

    def relay(c):
        move(c, 0).wait_recv()
        move(c, 4).start()
        move(c, 2).wait_recv()
        move(c, 5).start()

    def part(c, kind, shift=0):
        offset = (-1, 1, -1, -1, -3, -3, -RING, -RING)[kind] + shift
        return remote(tx.at[c, kind], rx.at[c, kind], send_part.at[kind, c], recv_part.at[kind, c], offset)

    def give(c, kind):
        turn = (0, 0, 0, 0, 2, 2)[kind]

        @pl.when(place == turn)
        def _():
            part(c, kind, RING).start()

        @pl.when(place != turn)
        def _():
            part(c, kind).start()

    def join(c):
        @pl.when(place == RING - 1)
        def _():
            for kind in (2, 4):
                part(c, kind).wait_recv()
            tx[c, 6] = (rx[c, 2].astype(F32) + rx[c, 4].astype(F32)).astype(BF16)
            part(c, 6).start()
            for kind in (3, 5):
                part(c, kind).wait_recv()
            tx[c, 7] = (rx[c, 3].astype(F32) + rx[c, 5].astype(F32)).astype(BF16)
            part(c, 7).start()

    ids_to(1, 0, 1).start()
    ids_to(3, 0, 3).start()
    feed(0)
    for c in range(1, kvs):
        split(c)
    ids_to(1, 0, 1).wait_recv()
    ids_to(2, 1, 1).start()
    forward(0)
    feed(1)
    relay(0)
    forward(1)
    feed(2)

    lanes = lax.broadcasted_iota(jnp.int32, (tok, width), 1).astype(F32)

    def column(slot):
        return jnp.transpose(jnp.broadcast_to(ids_in[slot].astype(F32), (width, tok)))

    hot[...] = jnp.where(column(0) == lanes, 1.0, 0.0).astype(BF16)
    ids_to(3, 0, 3).wait_recv()
    ids_to(2, 1, 1).wait_recv()
    for slot in range(4):
        blocked[block(slot)] = jnp.where(column(slot) == lanes, 0.0, BLOCKED).astype(BF16)
    low = lax.broadcasted_iota(jnp.int32, (half, half), 1) <= lax.broadcasted_iota(jnp.int32, (half, half), 0)
    keep = [jnp.where(low, 1.0, 0.0).astype(BF16), jnp.where(low, 0.0, 1.0).astype(BF16)]

    def corners(ref):
        for i in range(group):
            ref[i * tok:i * tok + half, half:tok] = jnp.zeros((half, half), BF16)
            ref[i * tok + half:(i + 1) * tok, 3 * tok:3 * tok + half] = jnp.zeros((half, half), BF16)

    corners(p_all)
    for c in range(kvs):
        corners(ds_all.at[c])

    def products(c, h, slot, step):
        q = jnp.concatenate([q_all[h], hot[...]], axis=1)
        g = g_all[h]
        for out, rows, right in (
            ((s_a, s_b)[slot], q, lambda o: jnp.concatenate([near[c, 0, block(o)], blocked[block(o)]], axis=1)),
            ((d_a, d_b)[slot], g, lambda o: near[c, 1, block(o)]),
        ):
            if step in (1, 2):
                out[:, step * tok:(step + 1) * tok] = contract(rows, right(step), 1, 1)
            if step == 0:
                own = contract(rows, right(0), 1, 1)
                third = contract(rows, right(3), 1, 1)
                out[:half, :half] = jnp.where(low, own[:half, :half], third[:half, :half])
                out[:half, half:tok] = third[:half, half:]
                out[half:, :half] = own[half:, :half]
                out[half:, half:tok] = jnp.where(low, own[half:, half:], third[half:, half:])

    steps = 8
    some = tok // steps

    def spread(ref, i, first, x):
        rows = slice(i * tok + first, i * tok + first + some)
        part_of = slice(first % half, first % half + some)
        ref[rows, tok:3 * tok] = x[:, tok:]
        if first < half:
            ref[rows, :half] = x[:, :half] * keep[0][part_of]
            ref[rows, 3 * tok:3 * tok + half] = x[:, :half] * keep[1][part_of]
            ref[rows, 3 * tok + half:] = x[:, half:tok]
        else:
            ref[rows, :half] = x[:, :half]
            ref[rows, half:tok] = x[:, half:tok] * keep[0][part_of]
            ref[rows, 3 * tok + half:] = x[:, half:tok] * keep[1][part_of]

    def softmax(c, h, i, step):
        first = step * some
        rows = slice(first, first + some)
        s = (s_a, s_b)[i % 2][rows]
        d = (d_a, d_b)[i % 2][rows]
        peak = jnp.max(s, axis=1, keepdims=True)
        p = jnp.exp2((s - peak) * (scale * LOG2E))
        inverse = 1.0 / jnp.sum(p, axis=1, keepdims=True)
        center = jnp.sum(p * d, axis=1, keepdims=True) * inverse
        spread(ds_all.at[c], i, first, (p * (d - center)).astype(BF16))
        spread(p_all, i, first, p.astype(BF16))
        inv_all[c, i * tok + first:i * tok + first + some] = jnp.broadcast_to(inverse, (some, width))
        if step == steps - 1:
            head = slice(i * tok, (i + 1) * tok)
            q_turned[:, head] = jnp.transpose(q_all[h].astype(F32) * inv_all[c, head]).astype(BF16)
            g_turned[:, head] = jnp.transpose(g_all[h].astype(F32) * inv_all[c, head]).astype(BF16)

    def query_part(c, h, i):
        head = slice(i * tok, (i + 1) * tok)
        dq[h] = (contract(ds_all[c, head], near[c, 0], 1, 0) * (inv_all[c, head] * scale)).astype(BF16)

    def key_part(c, slot):
        x = contract(q_turned[...], ds_all[c, :, slot * tok:(slot + 1) * tok], 1, 0)
        return jnp.transpose(x) * scale

    def value_part(slot):
        x = contract(g_turned[...], p_all[:, slot * tok:(slot + 1) * tok], 1, 0)
        return jnp.transpose(x)

    def interleave(*items):
        for step in range(steps):
            for work, args, number in items:
                for one in range(step * number // steps, (step + 1) * number // steps):
                    work(*args, one)

    def middle(c):
        part(c, 0).wait_recv()
        tx[c, 2] = (own_sum[c, 2] + rx[c, 0].astype(F32)).astype(BF16)
        give(c, 2)
        part(c, 1).wait_recv()
        tx[c, 5] = (own_sum[c, 3] + rx[c, 1].astype(F32)).astype(BF16)
        give(c, 5)

    def finish(c):
        def total(which, kinds):
            for kind in kinds:
                part(c, kind).wait_recv()
            x = rx[c, kinds[0]].astype(F32)
            for kind in kinds[1:]:
                x = x + rx[c, kind].astype(F32)
            rows32[which, pl.ds(c, tok, stride=kvs), :] = own_sum[c, which] + x

        @pl.when(place == RING - 1)
        def _():
            total(0, (6,))
            total(1, (7,))

        @pl.when(place != RING - 1)
        def _():
            total(0, (2, 4))
            total(1, (3, 5))

    def chunk(c, carry):
        for kind in (1, 3, 4, 5):
            move(c, kind).wait_recv()
        for copy in load(c):
            copy.wait()

        def first(i):
            return (products, (c, c * group + i, i % 2), 4)

        def second(i):
            return (softmax, (c, c * group + i, i), steps)

        events = ((3, 1, relay), (5, 2, forward), (5, 3, feed), (6, -1, middle), (6, -2, join))
        interleave(first(0))
        interleave(second(0), first(1))
        for i in range(2, group):
            for when, ahead, event in events:
                if when == i:
                    pl.when((c + ahead >= 0) & (c + ahead < kvs))(functools.partial(event, c + ahead))
            interleave(second(i - 1), first(i))
        interleave(second(group - 1))
        tx[c, 0] = key_part(c, 2).astype(BF16)
        part(c, 0).start()
        tx[c, 1] = value_part(2).astype(BF16)
        part(c, 1).start()
        tx[c, 3] = value_part(1).astype(BF16)
        give(c, 3)
        tx[c, 4] = key_part(c, 3).astype(BF16)
        give(c, 4)
        own_sum[c, 2] = key_part(c, 1)
        own_sum[c, 3] = value_part(3)
        own_sum[c, 0] = key_part(c, 0)
        own_sum[c, 1] = value_part(0)
        return carry

    def queries_of(c, carry):
        for i in range(group):
            query_part(c, c * group + i, i)
        return carry

    def ended(c, carry):
        finish(c)
        return carry

    lax.fori_loop(0, kvs, chunk, 0)
    lax.fori_loop(0, kvs // 4, queries_of, 0)
    join(kvs - 2)
    middle(kvs - 1)
    lax.fori_loop(kvs // 4, kvs, queries_of, 0)
    lax.fori_loop(0, kvs - 1, ended, 0)
    join(kvs - 1)
    finish(kvs - 1)

    def wrap_up(c, carry):
        for kind in range(6):
            move(c, kind).wait_send()
            part(c, kind).wait_send()

        @pl.when(place == RING - 1)
        def _():
            for which in range(2):
                onward(c, which).wait_send()
                part(c, 6 + which).wait_send()

        return carry

    lax.fori_loop(0, kvs, wrap_up, 0)
    ids_to(1, 0, 1).wait_send()
    ids_to(3, 0, 3).wait_send()
    ids_to(2, 1, 1).wait_send()
    dk_rows[...] = rows32[0].astype(BF16)
    dv_rows[...] = rows32[1].astype(BF16)


def shards(grps, ctxs, queries, key_rows, value_rows, out_grad, doc_ids):
    tok, heads, width = queries.shape
    kvs = key_rows.shape[1]
    group = heads // kvs
    vmem = pl.BlockSpec(memory_space=pltpu.VMEM)
    anywhere = pl.BlockSpec(memory_space=pl.ANY)
    dma = pltpu.SemaphoreType.DMA
    dq, dk, dv = pl.pallas_call(
        functools.partial(kernel, grps, ctxs, group, width ** -0.5),
        out_shape=(
            pltpu.VMEM((heads, tok, width), BF16),
            pltpu.VMEM((tok * kvs, width), BF16),
            pltpu.VMEM((tok * kvs, width), BF16),
        ),
        in_specs=[anywhere, anywhere, anywhere, anywhere, vmem],
        out_specs=[vmem, vmem, vmem],
        scratch_shapes=[
            pltpu.VMEM((heads, tok, width), BF16),
            pltpu.VMEM((heads, tok, width), BF16),
            pltpu.VMEM((tok * kvs, width), BF16),
            pltpu.VMEM((tok * kvs, width), BF16),
            pltpu.VMEM((2, tok * kvs, width), F32),
            pltpu.VMEM((kvs, 2, 4 * tok, width), BF16),
            pltpu.VMEM((4, 1, tok), jnp.int32),
            pltpu.VMEM((tok, width), BF16),
            pltpu.VMEM((4 * tok, width), BF16),
            pltpu.VMEM((tok, 3 * tok), F32),
            pltpu.VMEM((tok, 3 * tok), F32),
            pltpu.VMEM((tok, 3 * tok), F32),
            pltpu.VMEM((tok, 3 * tok), F32),
            pltpu.VMEM((kvs, group * tok, 4 * tok), BF16),
            pltpu.VMEM((group * tok, 4 * tok), BF16),
            pltpu.VMEM((width, group * tok), BF16),
            pltpu.VMEM((width, group * tok), BF16),
            pltpu.VMEM((kvs, group * tok, width), F32),
            pltpu.VMEM((kvs, 2, tok, width), BF16),
            pltpu.VMEM((kvs, 4, tok, width), F32),
            pltpu.VMEM((kvs, 8, tok, width), BF16),
            pltpu.VMEM((kvs, 8, tok, width), BF16),
            dma((kvs,)), dma((kvs,)), dma((2,)),
            dma((8, kvs)), dma((8, kvs)),
            dma((4,)), dma((4,)),
            dma((8, kvs)), dma((8, kvs)),
        ],
        compiler_params=pltpu.CompilerParams(
            collective_id=0, has_side_effects=True, vmem_limit_bytes=56 * 2**20
        ),
    )(
        jnp.transpose(queries, (1, 0, 2)),
        jnp.transpose(out_grad, (1, 0, 2)),
        key_rows.reshape(tok * kvs, width),
        value_rows.reshape(tok * kvs, width),
        doc_ids.reshape(1, tok),
    )
    return (
        jnp.transpose(dq, (1, 0, 2)),
        dk.reshape(tok, kvs, width),
        dv.reshape(tok, kvs, width),
    )


def solution(mesh):
    spec = P(AXES, None, None)
    return jax.shard_map(
        functools.partial(shards, mesh.shape["grp"], mesh.shape["ctx"]),
        mesh=mesh,
        in_specs=(spec, spec, spec, spec, P(AXES)),
        out_specs=(spec, spec, spec),
        check_vma=False,
    )
```
